32 devices in a mesh: wide: 16 (over z, y, x), narrow: 2 (over core).
Axes of the slice: x: 2, y: 2, z: 4, core: 2. Of those that a mesh axis runs over, the one named last changes fastest.
Arguments:
- tokens: bfloat16 [1024, 2, 5120], P('wide', None, 'narrow'), may hold values from -6 to 6
- qkv_weight: bfloat16 [5120, 6144], P('wide', 'narrow'), may hold values from -0.078125 to 0.078125
- rotated_prefix_keys: bfloat16 [16, 2048, 1024], P('wide', None, 'narrow'), may hold values from -120 to 120
- shared_prefix_values: bfloat16 [16, 2048, 1024], P('wide', None, 'narrow'), may hold values from -6 to 6
- prefix_of: int32 [1024, 1], P('wide'), may hold values from 0 to 15; in each aligned block of 64 rows (0 to 63, 64 to 127, ...) at most 8 rows name the same one
- positions: int32 [1024], P('wide'), may hold values from 512 to 2048, as said below
Outputs:
- attended: bfloat16 [1024, 2, 4096], P('wide', None, 'narrow')
The draws below stay inside these ranges and needn't reach their ends.
Inputs may be any that keep to these rules, and one draw needn't show every extreme that they name: `prefix_of`: the 64 requests of one index of wide name each prefix at most 8 times, a bound that some block reaches. The new tokens of request r sit at positions[r] + s.
All inputs are finite; a program needn't handle non-finite values.
Results may differ from the reference program's by a relative error of at most 0.012.
The reference program's roundings to bfloat16 on the way count: a program that leaves them out, or rounds other values in their place, can miss the bound.
Values may be sent and summed in bfloat16 or wider, within the bound.
No kernel may reach another device: no remote copies, remote signals or barrier semaphores. Data moves between devices by JAX's collectives and lax.ppermute only.
A program may use at most 128 MiB of HBM per device.

```python
import math
import jax
import jax.numpy as jnp
import numpy as np
from jax import lax

D = 5120
QUERY_HEADS = 32
KEY_VALUE_HEADS = 8
HEAD_SIZE = 128
PREFIX_LENGTH = 2048
R_DEV = 64
DECODE_STEPS = 2
CAP = 8
COLS = 6144
SHARED_PREFIXES = 16
REQUEST_COUNT = 1024


def draw_positions(key, part):
    counts = jax.random.randint(key, (REQUEST_COUNT,), PREFIX_LENGTH // 4, PREFIX_LENGTH + 1)
    return counts.at[0].set(PREFIX_LENGTH).astype(jnp.int32)


def draw_rotated_prefix_keys(key, part):
    first_index = jax.random.fold_in(key, 0)
    value_block = jax.random.normal(first_index, (SHARED_PREFIXES, PREFIX_LENGTH, KEY_VALUE_HEADS * HEAD_SIZE), jnp.float32)
    return jnp.clip(value_block, -120.0, 120.0).astype(jnp.bfloat16)


def block_scale(rng, dims, cuts, low, top_value):
    def one(position, parts):
        steps = jax.random.uniform(jax.random.fold_in(jax.random.fold_in(rng, 6), position), (parts,), jnp.float32, low / len(cuts), top_value / len(cuts))
        return jnp.repeat(jnp.exp(steps), dims[position] // parts).reshape((-1,) + (1,) * (len(dims) - position - 1))

    gain = one(*cuts[0])
    for cut in cuts[1:]:
        gain = gain * one(*cut)
    return gain


def shared_out(stream_key, own, number, rows, count, top, reach, lean):
    order = jax.random.permutation(stream_key, count)
    heavy_load, common = shares(count, rows * top, reach, lean, True), shares(count, rows * top, reach, lean, False)
    places = jnp.arange(count)

    def named(lengths, offset_by):
        used = int((lengths > 0).sum())
        fixed = max(1, used // 4)
        passed = fixed + (places - fixed + offset_by * (used - fixed)) % max(1, count - fixed)
        return jnp.zeros((count,), jnp.int32).at[order[jnp.where(places < fixed, places, passed)]].set(jnp.asarray(lengths, jnp.int32))

    lengths = jnp.where(number % 4 == 0, named(heavy_load, number // 4), named(common, number - number // 4 - 1))
    mixed = jax.random.permutation(jax.random.fold_in(own, 3), count)
    source_of, taker = mixed[0:count // 2 * 2:2], mixed[1:count // 2 * 2:2]
    slack = jnp.minimum(lengths[source_of] - 1, reach - lengths[taker]) // 2
    slack = jnp.where((source_of == order[0]) | (taker == order[0]) | (lengths[taker] == 0), 0, jnp.maximum(slack, 0))
    passed = jax.random.randint(jax.random.fold_in(own, 4), (count // 2,), 0, 1 << 20) % (slack + 1)
    lengths = lengths.at[source_of].add(-passed).at[taker].add(passed)
    items = jnp.searchsorted(jnp.cumsum(lengths), jnp.arange(rows * top), side="right").astype(jnp.int32)
    table = items.reshape(top, rows).T
    table = table[jax.random.permutation(jax.random.fold_in(own, 1), rows)]
    offset_by = jax.random.randint(jax.random.fold_in(own, 2), (rows, 1), 0, top)
    return jnp.take_along_axis(table, (jnp.arange(top)[None, :] + offset_by) % top, axis=1)


def shares(count, total, most, lean, full):
    portions = [(1 << 20) // math.isqrt(rank ** lean) + 1 for rank in range(1, count + 1)]
    largest = most if full else min(most, max(-(-total // count), total * portions[0] // sum(portions)))
    least = 1 if total - largest >= count - 1 else 0
    holding, spare = [largest] + [least] * (count - 1), total - largest - least * (count - 1)
    while spare > 0:
        movable = [i for i in range(1, count) if holding[i] < largest] or [i for i in range(1, count) if holding[i] < most]
        mass, remaining = sum([portions[i] for i in movable]), spare
        for i in movable:
            addition = min(most - holding[i], max(1, remaining * portions[i] // mass), spare)
            holding[i] = holding[i] + addition
            spare = spare - addition
    return np.array(holding)


def scatter_about(key, shape, scale, bound, cuts=(), held_as=jnp.bfloat16):
    values = jax.random.normal(key, shape, jnp.float32) * scale
    if len(cuts) > 0:
        values = block_scale(key, shape, cuts, -0.22, 0.18) * values
    return jnp.clip(values, min=-bound, max=bound).astype(held_as)


def setup_inputs(seed: int = 0) -> dict:
    key_list = jax.random.split(jax.random.key(seed), 7)
    tokens = scatter_about(key_list[0], (REQUEST_COUNT, DECODE_STEPS, D), 1.0, 6.0, ((0, 16), (2, 2)))
    qkv_weight = scatter_about(key_list[1], (D, COLS), D ** -0.5, 0.078125, ((0, 16), (1, 2)))
    rotated_prefix_keys = draw_rotated_prefix_keys(jax.random.fold_in(key_list[6], 71), 0)
    shared_prefix_values = scatter_about(key_list[3], (SHARED_PREFIXES, PREFIX_LENGTH, KEY_VALUE_HEADS * HEAD_SIZE), 1.0, 6.0, ((0, 16), (2, 2)))
    prefix_of_keys = jax.random.split(jax.random.fold_in(key_list[4], 1), REQUEST_COUNT // R_DEV)
    prefix_of_turns = jax.random.permutation(jax.random.fold_in(key_list[4], 3), REQUEST_COUNT // R_DEV)
    prefix_of = jax.vmap(lambda own, number: shared_out(jax.random.fold_in(key_list[4], 2), own, number, R_DEV, SHARED_PREFIXES, 1, CAP, 2))(prefix_of_keys, prefix_of_turns).reshape((REQUEST_COUNT, 1))
    positions = draw_positions(jax.random.fold_in(key_list[6], 71), 0)
    return {"tokens": tokens, "qkv_weight": qkv_weight, "rotated_prefix_keys": rotated_prefix_keys, "shared_prefix_values": shared_prefix_values, "prefix_of": prefix_of, "positions": positions}


def rotate(value_block, where):
    half = HEAD_SIZE // 2
    freq = 10000.0 ** (-(jnp.arange(half, dtype=jnp.float32) * 2.0 / HEAD_SIZE))
    angle = where[..., None].astype(jnp.float32) * freq
    cosine = jnp.cos(angle)
    sine = jnp.sin(angle)
    first_index = value_block[..., :half]
    second = value_block[..., half:]
    return jnp.concatenate([first_index * cosine - second * sine, second * cosine + first_index * sine], axis=-1)


def reference(tokens, qkv_weight, rotated_prefix_keys, shared_prefix_values, prefix_of, positions):
    query_group = QUERY_HEADS // KEY_VALUE_HEADS
    flat = tokens.reshape(REQUEST_COUNT * DECODE_STEPS, D)
    mixed_output = jnp.dot(flat, qkv_weight, preferred_element_type=jnp.float32)
    mixed_output = mixed_output.reshape(REQUEST_COUNT, DECODE_STEPS, KEY_VALUE_HEADS, query_group + 2, HEAD_SIZE)
    where = positions[:, None] + jnp.arange(DECODE_STEPS, dtype=jnp.int32)[None, :]
    query = rotate(mixed_output[:, :, :, :query_group, :], where[:, :, None, None]).astype(jnp.bfloat16)
    own_key = rotate(mixed_output[:, :, :, query_group, :], where[:, :, None]).astype(jnp.bfloat16)
    own_value = mixed_output[:, :, :, query_group + 1, :].astype(jnp.bfloat16)
    block_slice = 16
    scale = 1.0 / (HEAD_SIZE ** 0.5)

    def attend(index):
        start = (index * block_slice).astype(jnp.int32)
        q_block = lax.dynamic_slice_in_dim(query, start, block_slice, 0).astype(jnp.float32)
        k_block = lax.dynamic_slice_in_dim(own_key, start, block_slice, 0).astype(jnp.float32)
        v_block = lax.dynamic_slice_in_dim(own_value, start, block_slice, 0).astype(jnp.float32)
        chosen_prefix = lax.dynamic_slice_in_dim(prefix_of[:, 0], start, block_slice, 0)
        limit = lax.dynamic_slice_in_dim(positions, start, block_slice, 0)
        key_rows = jnp.take(rotated_prefix_keys, chosen_prefix, axis=0).reshape(block_slice, PREFIX_LENGTH, KEY_VALUE_HEADS, HEAD_SIZE).astype(jnp.float32)
        value_rows = jnp.take(shared_prefix_values, chosen_prefix, axis=0).reshape(block_slice, PREFIX_LENGTH, KEY_VALUE_HEADS, HEAD_SIZE).astype(jnp.float32)
        far = jnp.einsum("bskgd,blkd->bskgl", q_block, key_rows) * scale
        allowed = jnp.arange(PREFIX_LENGTH, dtype=jnp.int32)[None, :] < limit[:, None]
        far = jnp.where(allowed[:, None, None, None, :], far, -1e30)
        near = jnp.einsum("bskgd,btkd->bskgt", q_block, k_block) * scale
        causal = jnp.arange(DECODE_STEPS)[:, None] >= jnp.arange(DECODE_STEPS)[None, :]
        near = jnp.where(causal[None, :, None, None, :], near, -1e30)
        top = jnp.maximum(jnp.max(far, axis=-1), jnp.max(near, axis=-1))
        far_w = jnp.exp(far - top[..., None])
        near_w = jnp.exp(near - top[..., None])
        total = jnp.sum(far_w, axis=-1) + jnp.sum(near_w, axis=-1)
        far_b = lax.optimization_barrier(far_w.astype(jnp.bfloat16)).astype(jnp.float32)
        near_b = lax.optimization_barrier(near_w.astype(jnp.bfloat16)).astype(jnp.float32)
        summed = jnp.einsum("bskgl,blkd->bskgd", far_b, value_rows) + jnp.einsum("bskgt,btkd->bskgd", near_b, v_block)
        result = summed / total[..., None]
        return result.astype(jnp.bfloat16).reshape(block_slice, DECODE_STEPS, QUERY_HEADS * HEAD_SIZE)

    pieces = lax.map(attend, jnp.arange(REQUEST_COUNT // block_slice, dtype=jnp.int32))
    return pieces.reshape(REQUEST_COUNT, DECODE_STEPS, QUERY_HEADS * HEAD_SIZE)
```

```python
import functools

import jax
import jax.numpy as jnp
from jax import lax
from jax.experimental import pallas as pl
from jax.experimental.pallas import tpu as pltpu
from jax.sharding import PartitionSpec as P

QUERY_HEADS = 32
KEY_VALUE_HEADS = 8
HEAD_SIZE = 128
DECODE_STEPS = 2
GROUP = QUERY_HEADS // KEY_VALUE_HEADS
SCALE = 1.0 / HEAD_SIZE**0.5
FLOOR = 512
PIECES = 3
NT = (((1,), (1,)), ((), ()))
NN = (((1,), (0,)), ((), ()))


def dot(left, right, dims=NN):
    return lax.dot_general(left, right, dims, preferred_element_type=jnp.float32)


def whole_specs(count):
    return [pl.BlockSpec(memory_space=pltpu.VMEM)] * count


def prefix_kernel(tile, asked, limit, keys, values, out):
    rows = asked.shape[0]
    length = keys.shape[0]
    heads = keys.shape[1] // HEAD_SIZE
    bound = limit[...]
    lane = lax.broadcasted_iota(jnp.int32, (rows, HEAD_SIZE), 1)
    stat = jnp.zeros((rows, HEAD_SIZE), jnp.float32)
    for head in range(heads):
        key_at = slice(head * HEAD_SIZE, (head + 1) * HEAD_SIZE)
        for member in range(GROUP):
            column = head * GROUP + member
            at = slice(column * HEAD_SIZE, (column + 1) * HEAD_SIZE)
            query = asked[:, at]
            parts = []
            top = None
            for start in range(0, length, tile):
                score = dot(query, keys[start : start + tile, key_at], NT)
                if start + tile > FLOOR:
                    where = start + lax.broadcasted_iota(jnp.int32, score.shape, 1)
                    score = jnp.where(where < bound, score, -1e30)
                parts.append(score)
                high = jnp.max(score, axis=1, keepdims=True)
                top = high if top is None else jnp.maximum(top, high)
            total = jnp.zeros((rows, 1), jnp.float32)
            summed = jnp.zeros((rows, HEAD_SIZE), jnp.float32)
            for index, start in enumerate(range(0, length, tile)):
                weight = jnp.exp((parts[index] - top) * SCALE)
                total = total + jnp.sum(weight, axis=1, keepdims=True)
                summed = summed + dot(
                    weight.astype(jnp.bfloat16), values[start : start + tile, key_at]
                )
            out[:, at] = (summed / total).astype(jnp.bfloat16)
            left = top * SCALE + jnp.log(total)
            for piece in range(PIECES):
                part = left.astype(jnp.bfloat16).astype(jnp.float32)
                stat = jnp.where(lane == piece * heads * GROUP + column, part, stat)
                left = left - part
    out[:, heads * GROUP * HEAD_SIZE :] = stat.astype(jnp.bfloat16)


def prefix_part(asked, limit, keys, values, first, heads):
    rows, width = asked.shape
    length = keys.shape[0]
    block = pl.BlockSpec((length, heads * HEAD_SIZE), lambda i: (0, first // heads))
    return pl.pallas_call(
        functools.partial(prefix_kernel, min(length, 512)),
        grid=(1,),
        out_shape=jax.ShapeDtypeStruct((rows, width + HEAD_SIZE), jnp.bfloat16),
        in_specs=[
            pl.BlockSpec((rows, width), lambda i: (0, 0)),
            pl.BlockSpec((rows, 1), lambda i: (0, 0)),
            block,
            block,
        ],
        out_specs=pl.BlockSpec((rows, width + HEAD_SIZE), lambda i: (0, 0)),
        compiler_params=pltpu.CompilerParams(vmem_limit_bytes=40 * 2**20),
        cost_estimate=pl.CostEstimate(
            flops=4 * rows * length * width,
            bytes_accessed=4 * length * heads * HEAD_SIZE,
            transcendentals=rows * length * heads * GROUP,
        ),
        name="prefix_part",
    )(asked, limit, keys, values)


def pack_kernel(count, *refs):
    parts, (cosine, sine, route, asked, query, key, value) = refs[:count], refs[count:]
    heads = key.shape[1] // HEAD_SIZE

    def column(index):
        at = slice(index * HEAD_SIZE, (index + 1) * HEAD_SIZE)
        total = parts[0][:, at].astype(jnp.float32)
        for part in parts[1:]:
            total = total + part[:, at].astype(jnp.float32)
        return total

    def rotated(block):
        turned = pltpu.roll(block, HEAD_SIZE // 2, 1)
        return (block * cosine[...] + turned * sine[...]).astype(jnp.bfloat16)

    for head in range(heads):
        base = head * (GROUP + 2)
        for member in range(GROUP):
            at = head * GROUP + member
            query[:, at * HEAD_SIZE : (at + 1) * HEAD_SIZE] = rotated(column(base + member))
        at = slice(head * HEAD_SIZE, (head + 1) * HEAD_SIZE)
        key[:, at] = rotated(column(base + GROUP))
        value[:, at] = column(base + GROUP + 1).astype(jnp.bfloat16)
    asked[...] = dot(route[...], query[...]).astype(jnp.bfloat16)


def pack(parts, cosine, sine, route, heads):
    rows = cosine.shape[0]
    slots = route.shape[0]
    wide_q, wide_k = heads * GROUP * HEAD_SIZE, heads * HEAD_SIZE
    return pl.pallas_call(
        functools.partial(pack_kernel, len(parts)),
        out_shape=[
            jax.ShapeDtypeStruct((slots, wide_q), jnp.bfloat16),
            jax.ShapeDtypeStruct((rows, wide_q), jnp.bfloat16),
            jax.ShapeDtypeStruct((rows, wide_k), jnp.bfloat16),
            jax.ShapeDtypeStruct((rows, wide_k), jnp.bfloat16),
        ],
        in_specs=whole_specs(len(parts) + 3),
        out_specs=whole_specs(4),
        compiler_params=pltpu.CompilerParams(vmem_limit_bytes=24 * 2**20),
        cost_estimate=pl.CostEstimate(
            flops=2 * slots * rows * wide_q, bytes_accessed=8 * rows * wide_q, transcendentals=0
        ),
        name="pack",
    )(*parts, cosine, sine, route)


def join_kernel(back, route, query, key, value, out):
    rows = query.shape[0]
    heads = key.shape[1] // HEAD_SIZE
    far = dot(route[...], back[...], (((0,), (0,)), ((), ())))
    stat = far[:, heads * GROUP * HEAD_SIZE :]
    row = lax.broadcasted_iota(jnp.int32, (rows, rows), 0)
    other = lax.broadcasted_iota(jnp.int32, (rows, rows), 1)
    allowed = (row // DECODE_STEPS == other // DECODE_STEPS) & (other <= row)
    for head in range(heads):
        own = slice(head * HEAD_SIZE, (head + 1) * HEAD_SIZE)
        for member in range(GROUP):
            column = head * GROUP + member
            at = slice(column * HEAD_SIZE, (column + 1) * HEAD_SIZE)
            score = jnp.where(allowed, dot(query[:, at], key[:, own], NT) * SCALE, -1e30)
            top = jnp.max(score, axis=1, keepdims=True)
            weight = jnp.exp(score - top)
            total = jnp.sum(weight, axis=1, keepdims=True)
            near = dot(weight.astype(jnp.bfloat16), value[:, own])
            level = jnp.zeros((rows, 1), jnp.float32)
            for piece in range(PIECES):
                lane = piece * heads * GROUP + column
                level = level + stat[:, lane : lane + 1]
            both = jnp.maximum(level, top)
            left = jnp.exp(level - both)
            right = jnp.exp(top - both)
            merged = (far[:, at] * left + near * right) / (left + total * right)
            out[:, at] = merged.astype(jnp.bfloat16)


def join(back, route, query, key, value):
    return pl.pallas_call(
        join_kernel,
        out_shape=jax.ShapeDtypeStruct(query.shape, jnp.bfloat16),
        in_specs=whole_specs(5),
        out_specs=whole_specs(1)[0],
        compiler_params=pltpu.CompilerParams(vmem_limit_bytes=24 * 2**20),
        cost_estimate=pl.CostEstimate(
            flops=2 * route.shape[0] * route.shape[1] * back.shape[1],
            bytes_accessed=8 * query.shape[0] * query.shape[1],
            transcendentals=0,
        ),
        name="join",
    )(back, route, query, key, value)


def inner_size(owners):
    return 4 if owners % 4 == 0 else 1


def across(block, mask, owners):
    return lax.ppermute(block, "wide", [(i, i ^ mask) for i in range(owners)])


def plane_rows(piece, owners):
    if inner_size(owners) == 1:
        return piece
    half = piece.shape[0] // 2
    upper, lower = piece[:half], piece[half:]
    upper_1 = across(upper, 1, owners)
    lower_2 = across(lower, 2, owners)
    upper_2 = across(upper, 2, owners)
    lower_1 = across(lower, 1, owners)
    upper_3 = across(upper_1, 2, owners)
    lower_3 = across(lower_2, 1, owners)
    return jnp.concatenate(
        [upper, lower, upper_1, lower_1, upper_2, lower_2, upper_3, lower_3], axis=0
    )


def line_groups(owners, inner):
    return [[i * inner + j for i in range(owners // inner)] for j in range(inner)]


def line_tokens(tokens, owners, inner, halves):
    planes = owners // inner
    rows = tokens.shape[0] * tokens.shape[1]
    flat = tokens.reshape(rows, tokens.shape[2])
    if halves == 2:
        other = lax.ppermute(flat, "narrow", [(0, 1), (1, 0)])
        first = lax.axis_index("narrow") == 0
        flat = jnp.concatenate([jnp.where(first, flat, other), jnp.where(first, other, flat)], 1)
    else:
        flat = lax.all_gather(flat, "narrow", axis=1, tiled=True)
    if planes > 1:
        parts = flat.reshape(rows, planes, -1).transpose(1, 0, 2)
        parts = lax.all_to_all(
            parts, "wide", split_axis=0, concat_axis=0, tiled=True,
            axis_index_groups=line_groups(owners, inner),
        )
        flat = parts.reshape(planes * rows, -1)
    here = lax.axis_index("wide") % inner
    split = flat.reshape(planes * rows, inner, -1)
    return jnp.concatenate(
        [lax.dynamic_index_in_dim(split, here ^ j, 1, keepdims=False) for j in range(inner)], axis=1
    )


def line_sums(partial, owners, inner):
    planes = owners // inner
    if planes == 1:
        return [partial]
    rows = partial.shape[0] // planes
    parts = lax.all_to_all(
        partial.reshape(planes, rows, -1), "wide", split_axis=0, concat_axis=0, tiled=True,
        axis_index_groups=line_groups(owners, inner),
    )
    return [parts[i] for i in range(planes)]


def exchange(block):
    return lax.all_to_all(block, "wide", split_axis=0, concat_axis=0, tiled=True)


def on_device(tokens, qkv_weight, rotated_prefix_keys, shared_prefix_values, prefix_of, positions):
    rows_dev = tokens.shape[0]
    owners = lax.axis_size("wide")
    halves = lax.axis_size("narrow")
    inner = inner_size(owners)
    rows = rows_dev * DECODE_STEPS
    capacity = max(2, (2 * rows_dev + owners - 1) // owners)
    slots = owners * capacity
    kv_local = rotated_prefix_keys.shape[2] // HEAD_SIZE
    chunks = 2 if kv_local % 2 == 0 else 1
    heads = kv_local // chunks
    columns = heads * (GROUP + 2) * HEAD_SIZE

    gathered = [
        plane_rows(qkv_weight[:, i * columns : (i + 1) * columns], owners) for i in range(chunks)
    ]
    inputs = line_tokens(tokens, owners, inner, halves)

    chosen = prefix_of[:, 0]
    hits = (chosen[:, None] == jnp.arange(owners, dtype=jnp.int32)[None, :]).astype(jnp.int32)
    rank = jnp.sum((jnp.cumsum(hits, axis=0) - hits) * hits, axis=1)
    target = chosen * capacity + rank
    dispatch = target[None, :] == jnp.arange(slots, dtype=jnp.int32)[:, None]
    limits = jnp.sum(jnp.where(dispatch, positions[None, :], 0), axis=1)
    bounds = exchange(limits.reshape(owners, capacity)).reshape(slots)
    bounds = jnp.repeat(bounds, DECODE_STEPS)[:, None]
    step = jnp.arange(DECODE_STEPS, dtype=jnp.int32)
    line = (target[:, None] * DECODE_STEPS + step[None, :]).reshape(rows)
    route = (
        line[None, :] == jnp.arange(slots * DECODE_STEPS, dtype=jnp.int32)[:, None]
    ).astype(jnp.bfloat16)

    half = HEAD_SIZE // 2
    freq = 10000.0 ** (-(jnp.arange(half, dtype=jnp.float32) * 2.0 / HEAD_SIZE))
    where = (positions[:, None] + step[None, :]).reshape(rows)
    angle = where[:, None].astype(jnp.float32) * freq
    cosine, sine = jnp.cos(angle), jnp.sin(angle)
    cosine = jnp.concatenate([cosine, cosine], axis=1)
    sine = jnp.concatenate([-sine, sine], axis=1)

    key_rows = rotated_prefix_keys[0]
    value_rows = shared_prefix_values[0]
    results = []
    for i in range(chunks):
        partial = dot(inputs, gathered[i]).astype(jnp.bfloat16)
        parts = line_sums(partial, owners, inner)
        packed, query, own_key, own_value = pack(parts, cosine, sine, route, heads)
        width = packed.shape[1]
        asked = exchange(packed.reshape(owners, capacity * DECODE_STEPS, width))
        asked = asked.reshape(slots * DECODE_STEPS, width)
        far = prefix_part(asked, bounds, key_rows, value_rows, i * heads, heads)
        back = exchange(far.reshape(owners, capacity * DECODE_STEPS, -1))
        back = back.reshape(slots * DECODE_STEPS, -1)
        results.append(join(back, route, query, own_key, own_value))
    return jnp.concatenate(results, axis=1).reshape(rows_dev, DECODE_STEPS, -1)


def solution(mesh):
    return jax.shard_map(
        on_device,
        mesh=mesh,
        in_specs=(
            P("wide", None, "narrow"),
            P("wide", "narrow"),
            P("wide", None, "narrow"),
            P("wide", None, "narrow"),
            P("wide", None),
            P("wide"),
        ),
        out_specs=P("wide", None, "narrow"),
        check_vma=False,
    )
```

```python
import functools

import jax
import jax.numpy as jnp
from jax import lax
from jax.experimental import pallas as pl
from jax.experimental.pallas import tpu as pltpu
from jax.sharding import PartitionSpec as P

QUERY_HEADS = 32
KEY_VALUE_HEADS = 8
HEAD_SIZE = 128
DECODE_STEPS = 2
GROUP = QUERY_HEADS // KEY_VALUE_HEADS
SCALE = 1.0 / HEAD_SIZE**0.5
LOG2E = 1.4426950408889634
FLOOR = 512
RS = ("relay2", "relay2")
FARGATE = True
P2GATE = False
PROJ_MB = 40
TINY0 = True
TINY1 = False
SETTLE = 20000000
KP = 1.0
KA = 1.0
PGATE = False
KVLATE = False
CHUNKS = (2, 2)
PIECES = 3
NT = (((1,), (1,)), ((), ()))
NN = (((1,), (0,)), ((), ()))


def dot(left, right, dims=NN):
    return lax.dot_general(left, right, dims, preferred_element_type=jnp.float32)


def whole_specs(count):
    return [pl.BlockSpec(memory_space=pltpu.VMEM)] * count


def prefix_kernel(tile, heads, asked, marks, keys, values, out):
    rows = asked.shape[0]
    length = keys.shape[0]
    head = pl.program_id(0)
    wide = heads * GROUP * HEAD_SIZE
    bound = (marks[:, 0:1].astype(jnp.float32) + marks[:, 1:2].astype(jnp.float32)).astype(jnp.int32)
    lane = lax.broadcasted_iota(jnp.int32, (rows, HEAD_SIZE), 1)

    @pl.when(head == 0)
    def _():
        out[:, wide:] = jnp.zeros((rows, HEAD_SIZE), out.dtype)

    stat = out[:, wide:].astype(jnp.float32)
    ones = jnp.ones((tile, HEAD_SIZE), jnp.bfloat16)
    for member in range(GROUP):
        column = head * GROUP + member
        at = pl.ds(pl.multiple_of(column * HEAD_SIZE, HEAD_SIZE), HEAD_SIZE)
        query = asked[:, at]
        parts = []
        top = None
        for start in range(0, length, tile):
            score = dot(query, keys[start : start + tile, :], NT)
            if start + tile > FLOOR:
                where = start + lax.broadcasted_iota(jnp.int32, score.shape, 1)
                score = jnp.where(where < bound, score, -1e30)
            parts.append(score)
            high = jnp.max(score, axis=1, keepdims=True)
            top = high if top is None else jnp.maximum(top, high)
        total = jnp.zeros((rows, 1), jnp.float32)
        summed = jnp.zeros((rows, HEAD_SIZE), jnp.float32)
        for index, start in enumerate(range(0, length, tile)):
            weight = jnp.exp2((parts[index] - top) * (SCALE * LOG2E)).astype(jnp.bfloat16)
            both = dot(weight, jnp.concatenate([values[start : start + tile, :], ones], axis=1))
            summed = summed + both[:, :HEAD_SIZE]
            total = total + both[:, HEAD_SIZE : HEAD_SIZE + 1]
        out[:, at] = (summed / total).astype(jnp.bfloat16)
        left = top * SCALE + jnp.log(total)
        for piece in range(PIECES):
            part = left.astype(jnp.bfloat16).astype(jnp.float32)
            stat = jnp.where(lane == piece * heads * GROUP + column, part, stat)
            left = left - part
    out[:, wide:] = stat.astype(jnp.bfloat16)


def prefix_part(asked, marks, keys, values, first, heads):
    rows = asked.shape[0]
    length = keys.shape[0]
    wide = heads * GROUP * HEAD_SIZE
    last = marks.shape[1] // HEAD_SIZE - 1
    block = pl.BlockSpec((length, HEAD_SIZE), lambda i: (0, first + i))
    return pl.pallas_call(
        functools.partial(prefix_kernel, min(length, 512), heads),
        grid=(heads,),
        out_shape=jax.ShapeDtypeStruct((rows, wide + HEAD_SIZE), jnp.bfloat16),
        in_specs=[
            pl.BlockSpec((rows, wide), lambda i: (0, 0)),
            pl.BlockSpec((rows, HEAD_SIZE), lambda i: (0, last)),
            block,
            block,
        ],
        out_specs=pl.BlockSpec((rows, wide + HEAD_SIZE), lambda i: (0, 0)),
        compiler_params=pltpu.CompilerParams(vmem_limit_bytes=56 * 2**20),
        cost_estimate=pl.CostEstimate(
            flops=int(KA * 4 * rows * length * wide),
            bytes_accessed=4 * length * heads * HEAD_SIZE,
            transcendentals=rows * length * heads * GROUP,
        ),
        name="prefix_part",
    )(asked, marks, keys, values)


def pack_kernel(count, *refs):
    parts, (cosine, sine, route, marks, asked, query, key, value) = refs[:count], refs[count:]
    heads = key.shape[1] // HEAD_SIZE

    def column(index):
        at = slice(index * HEAD_SIZE, (index + 1) * HEAD_SIZE)
        total = parts[0][:, at].astype(jnp.float32)
        for part in parts[1:]:
            total = total + part[:, at].astype(jnp.float32)
        return total

    def rotated(block):
        turned = pltpu.roll(block, HEAD_SIZE // 2, 1)
        return (block * cosine[...] + turned * sine[...]).astype(jnp.bfloat16)

    for head in range(heads):
        base = head * (GROUP + 2)
        for member in range(GROUP):
            at = head * GROUP + member
            query[:, at * HEAD_SIZE : (at + 1) * HEAD_SIZE] = rotated(column(base + member))
        at = slice(head * HEAD_SIZE, (head + 1) * HEAD_SIZE)
        key[:, at] = rotated(column(base + GROUP))
        value[:, at] = column(base + GROUP + 1).astype(jnp.bfloat16)
    wide = query.shape[1]
    asked[:, :wide] = dot(route[...], query[...]).astype(jnp.bfloat16)
    if asked.shape[1] > wide:
        asked[:, wide:] = dot(route[...], marks[...]).astype(jnp.bfloat16)


def pack(parts, cosine, sine, route, marks, heads, marked):
    rows = cosine.shape[0]
    slots = route.shape[0]
    wide_q, wide_k = heads * GROUP * HEAD_SIZE, heads * HEAD_SIZE
    return pl.pallas_call(
        functools.partial(pack_kernel, len(parts)),
        out_shape=[
            jax.ShapeDtypeStruct((slots, wide_q + marked * HEAD_SIZE), jnp.bfloat16),
            jax.ShapeDtypeStruct((rows, wide_q), jnp.bfloat16),
            jax.ShapeDtypeStruct((rows, wide_k), jnp.bfloat16),
            jax.ShapeDtypeStruct((rows, wide_k), jnp.bfloat16),
        ],
        in_specs=whole_specs(len(parts) + 4),
        out_specs=whole_specs(4),
        compiler_params=pltpu.CompilerParams(vmem_limit_bytes=24 * 2**20),
        cost_estimate=pl.CostEstimate(
            flops=2 * slots * rows * wide_q, bytes_accessed=8 * rows * wide_q, transcendentals=0
        ),
        name="pack",
    )(*parts, cosine, sine, route, marks)


def near_kernel(query, key, value, summed, stat):
    rows = query.shape[0]
    heads = key.shape[1] // HEAD_SIZE
    lane = lax.broadcasted_iota(jnp.int32, (rows, HEAD_SIZE), 1)
    kept = jnp.zeros((rows, HEAD_SIZE), jnp.float32)
    row = lax.broadcasted_iota(jnp.int32, (rows, rows), 0)
    other = lax.broadcasted_iota(jnp.int32, (rows, rows), 1)
    allowed = (row // DECODE_STEPS == other // DECODE_STEPS) & (other <= row)
    for head in range(heads):
        own = slice(head * HEAD_SIZE, (head + 1) * HEAD_SIZE)
        for member in range(GROUP):
            column = head * GROUP + member
            at = slice(column * HEAD_SIZE, (column + 1) * HEAD_SIZE)
            score = jnp.where(allowed, dot(query[:, at], key[:, own], NT) * SCALE, -1e30)
            top = jnp.max(score, axis=1, keepdims=True)
            weight = jnp.exp(score - top)
            total = jnp.sum(weight, axis=1, keepdims=True)
            summed[:, at] = dot(weight.astype(jnp.bfloat16), value[:, own])
            kept = jnp.where(lane == column, top, kept)
            kept = jnp.where(lane == heads * GROUP + column, total, kept)
    stat[...] = kept


def near_part(query, key, value):
    rows, wide = query.shape
    return pl.pallas_call(
        near_kernel,
        out_shape=[
            jax.ShapeDtypeStruct((rows, wide), jnp.float32),
            jax.ShapeDtypeStruct((rows, HEAD_SIZE), jnp.float32),
        ],
        in_specs=whole_specs(3),
        out_specs=whole_specs(2),
        compiler_params=pltpu.CompilerParams(vmem_limit_bytes=24 * 2**20),
        cost_estimate=pl.CostEstimate(
            flops=4 * rows * rows * wide, bytes_accessed=8 * rows * wide, transcendentals=0
        ),
        name="near_part",
    )(query, key, value)


def join_kernel(back, route, summed, stat, out):
    wide = summed.shape[1]
    columns = wide // HEAD_SIZE
    far = dot(route[...], back[...], (((0,), (0,)), ((), ())))
    marks = far[:, wide:]
    for column in range(columns):
        at = slice(column * HEAD_SIZE, (column + 1) * HEAD_SIZE)
        level = marks[:, column : column + 1]
        for piece in range(1, PIECES):
            lane = piece * columns + column
            level = level + marks[:, lane : lane + 1]
        top = stat[:, column : column + 1]
        total = stat[:, columns + column : columns + column + 1]
        both = jnp.maximum(level, top)
        left = jnp.exp(level - both)
        right = jnp.exp(top - both)
        merged = (far[:, at] * left + summed[:, at] * right) / (left + total * right)
        out[:, at] = merged.astype(jnp.bfloat16)


def join(back, route, summed, stat):
    return pl.pallas_call(
        join_kernel,
        out_shape=jax.ShapeDtypeStruct(summed.shape, jnp.bfloat16),
        in_specs=whole_specs(4),
        out_specs=whole_specs(1)[0],
        compiler_params=pltpu.CompilerParams(vmem_limit_bytes=24 * 2**20),
        cost_estimate=pl.CostEstimate(
            flops=2 * route.shape[0] * route.shape[1] * back.shape[1],
            bytes_accessed=8 * summed.shape[0] * summed.shape[1],
            transcendentals=0,
        ),
        name="join",
    )(back, route, summed, stat)


def project_kernel(index, *refs):
    pieces, mine, other, outs, (rows, weight) = (
        refs[:8], refs[8:12], refs[12:16], refs[-6:-2], refs[-2:]
    )
    half, columns = pieces[0].shape
    size = mine[0].shape[0]
    place, end, holder = index[0], index[1], index[2]
    for i, piece in enumerate(pieces):
        start = (place ^ (i // 2)) * (2 * half) + (i % 2) * half
        weight[pl.ds(pl.multiple_of(start, 16), half), :] = piece[...]

    def fill(source):
        rows[:size] = source[0][...]
        rows[3 * size :] = source[2][...]

        @pl.when(end == 1)
        def _():
            rows[size : 2 * size] = source[3][...]
            rows[2 * size : 3 * size] = source[1][...]

        @pl.when(end == 0)
        def _():
            rows[size : 2 * size] = source[1][...]
            rows[2 * size : 3 * size] = source[3][...]

    @pl.when(holder == 1)
    def _():
        fill(mine)

    @pl.when(holder == 0)
    def _():
        fill(other)

    tile = 256
    for start in range(0, columns, tile):
        result = dot(rows[...], weight[:, start : start + tile]).astype(jnp.bfloat16)
        for i, out in enumerate(outs):
            out[:, start : start + tile] = result[i * size : (i + 1) * size]


def settle_kernel(*refs):
    refs[-1][...] = jnp.zeros_like(refs[-1])


def settle(arrived, size):
    return pl.pallas_call(
        settle_kernel,
        out_shape=jax.ShapeDtypeStruct((8, HEAD_SIZE), jnp.float32),
        in_specs=[pl.BlockSpec(memory_space=pl.ANY)] * len(arrived),
        out_specs=pl.BlockSpec(memory_space=pltpu.VMEM),
        cost_estimate=pl.CostEstimate(flops=0, bytes_accessed=size, transcendentals=0),
        name="settle",
    )(*arrived)


def project(index, pieces, mine, other, marks):
    columns = pieces[0].shape[1]
    size, depth = mine[0].shape
    return pl.pallas_call(
        project_kernel,
        out_shape=[jax.ShapeDtypeStruct((size, columns), jnp.bfloat16)] * 4,
        in_specs=[pl.BlockSpec(memory_space=pltpu.SMEM)]
        + whole_specs(16)
        + [pl.BlockSpec(memory_space=pl.ANY)] * len(marks),
        out_specs=whole_specs(4),
        scratch_shapes=[
            pltpu.VMEM((4 * size, depth), jnp.bfloat16),
            pltpu.VMEM((depth, columns), jnp.bfloat16),
        ],
        compiler_params=pltpu.CompilerParams(vmem_limit_bytes=PROJ_MB * 2**20),
        cost_estimate=pl.CostEstimate(
            flops=int(KP * 8 * size * depth * columns), bytes_accessed=2 * depth * columns, transcendentals=0
        ),
        name="project",
    )(index, *pieces, *mine, *other, *marks)


def after(value, *done):
    return lax.optimization_barrier((value, *done))[0]


def passed_on(source):
    return lax.ppermute(source[:16, :HEAD_SIZE], "narrow", [(0, 1), (1, 0)])[:1, :1]


def behind(value, mark):
    return jnp.where(mark == mark, value, 0).astype(value.dtype)


def inner_size(owners):
    return 4 if owners % 4 == 0 else 1


def across(block, mask, owners):
    return lax.ppermute(block, "wide", [(i, i ^ mask) for i in range(owners)])


def first_round(piece, owners, gate):
    half = piece.shape[0] // 2
    upper, lower = piece[:half], piece[half:]
    if gate is not None:
        upper, lower = after((upper, lower), *gate)
    return [upper, lower, across(upper, 1, owners), across(lower, 2, owners)]


def second_round(blocks, owners):
    upper, lower, upper_1, lower_2 = lax.optimization_barrier(blocks) if P2GATE else blocks
    upper_2, lower_1 = across(upper, 2, owners), across(lower, 1, owners)
    upper_3, lower_3 = across(upper_1, 2, owners), across(lower_2, 1, owners)
    return [upper, lower, upper_1, lower_1, upper_2, lower_2, upper_3, lower_3]


def line_groups(owners, inner):
    return [[i * inner + j for i in range(owners // inner)] for j in range(inner)]


def line_tokens(tokens, owners, inner, gate):
    plane = lax.axis_index("wide") // inner
    rows = tokens.shape[0] * tokens.shape[1]
    flat = tokens.reshape(rows, tokens.shape[2])
    if gate is not None:
        flat = behind(flat, gate)
    width = flat.shape[1] // 2
    even = plane % 2 == 0
    same = jnp.where(even, flat[:, :width], flat[:, width:])
    swap = jnp.where(even, flat[:, width:], flat[:, :width])
    blocks = [same]
    for mask, block in ((1, swap), (2, same), (3, swap)):
        pairs = []
        for owner in range(owners):
            there = owner ^ (mask * inner)
            core = there // inner // 2
            pairs.append((owner * 2 + core, there * 2 + core))
        blocks.append(lax.ppermute(block, ("wide", "narrow"), pairs))
    return blocks


def from_other_core(blocks):
    return [lax.ppermute(block, "narrow", [(0, 1), (1, 0)]) for block in blocks]


def line_sums(partial, owners, inner, how):
    own, first, second, third = partial
    plane = lax.axis_index("wide") // inner
    end = (plane == 0) | (plane == 3)

    def along(block, hops):
        pairs = [(a * inner + j, b * inner + j) for a, b in hops for j in range(inner)]
        return lax.ppermute(block, "wide", pairs)

    if how == "direct":
        near = along(first, [(0, 1), (1, 0), (2, 3), (3, 2)])
        mid = along(second, [(0, 3), (3, 0), (1, 2), (2, 1)])
        far = along(third, [(0, 2), (2, 0), (1, 3), (3, 1)])
        return [own, near, mid, far]
    near = along(first, [(0, 1), (1, 0), (2, 3), (3, 2)])
    middle = along(second, [(1, 2), (2, 1)])
    if how == "relay2":
        near, middle, second = lax.optimization_barrier((near, middle, second))
    outer = along(second, [(0, 1), (3, 2)])
    passed = jnp.where(end, 0, near.astype(jnp.float32))
    third = (third.astype(jnp.float32) + passed).astype(jnp.bfloat16)
    far = along(third, [(0, 2), (2, 0), (1, 3), (3, 1)])
    near = jnp.where(end, near, 0)
    return [own, near, outer, middle, far]


def project_any(tokens, qkv_weight, owners, inner):
    planes = owners // inner
    rows = tokens.shape[0] * tokens.shape[1]
    flat = lax.all_gather(tokens.reshape(rows, -1), "narrow", axis=1, tiled=True)
    weight = qkv_weight
    if inner > 1:
        groups = [[i * inner + j for j in range(inner)] for i in range(planes)]
        weight = lax.all_gather(weight, "wide", axis=0, tiled=True, axis_index_groups=groups)
    if planes == 1:
        return [dot(flat, weight)]
    lines = line_groups(owners, inner)
    parts = flat.reshape(rows, planes, -1).transpose(1, 0, 2)
    parts = lax.all_to_all(
        parts, "wide", split_axis=0, concat_axis=0, tiled=True, axis_index_groups=lines
    )
    partial = dot(parts.reshape(planes * rows, -1), weight).astype(jnp.bfloat16)
    parts = lax.all_to_all(
        partial.reshape(planes, rows, -1), "wide", split_axis=0, concat_axis=0, tiled=True,
        axis_index_groups=lines,
    )
    return [parts[i] for i in range(planes)]


def exchange(block):
    return lax.all_to_all(block, "wide", split_axis=0, concat_axis=0, tiled=True)


def on_device(tokens, qkv_weight, rotated_prefix_keys, shared_prefix_values, prefix_of, positions):
    rows_dev = tokens.shape[0]
    owners = lax.axis_size("wide")
    halves = lax.axis_size("narrow")
    inner = inner_size(owners)
    rows = rows_dev * DECODE_STEPS
    capacity = max(2, (2 * rows_dev + owners - 1) // owners)
    slots = owners * capacity
    kv_local = rotated_prefix_keys.shape[2] // HEAD_SIZE
    chunks = CHUNKS if sum(CHUNKS) == kv_local else (kv_local,)
    firsts = [sum(chunks[:i]) for i in range(len(chunks))]
    unit = (GROUP + 2) * HEAD_SIZE
    here = lax.axis_index("wide")
    plane = here // inner
    staged = owners == 4 * inner and inner == 4 and halves == 2

    if staged:
        def weight_columns(i):
            return qkv_weight[:, firsts[i] * unit : (firsts[i] + chunks[i]) * unit]

        started = first_round(weight_columns(0), owners, None)
        mine = line_tokens(tokens, owners, inner, passed_on(started[0]) if TINY0 else None)
        weights, other = second_round(started, owners), from_other_core(mine)
        index = jnp.stack(
            [
                here % inner,
                ((plane == 0) | (plane == 3)).astype(jnp.int32),
                (lax.axis_index("narrow") == plane // 2).astype(jnp.int32),
            ]
        ).astype(jnp.int32)

    chosen = prefix_of[:, 0]
    hits = (chosen[:, None] == jnp.arange(owners, dtype=jnp.int32)[None, :]).astype(jnp.int32)
    rank = jnp.sum((jnp.cumsum(hits, axis=0) - hits) * hits, axis=1)
    target = chosen * capacity + rank
    step = jnp.arange(DECODE_STEPS, dtype=jnp.int32)
    line = (target[:, None] * DECODE_STEPS + step[None, :]).reshape(rows)
    route = (
        line[None, :] == jnp.arange(slots * DECODE_STEPS, dtype=jnp.int32)[:, None]
    ).astype(jnp.bfloat16)

    count = jnp.repeat(positions, DECODE_STEPS)
    marks = jnp.stack([count - count % HEAD_SIZE, count % HEAD_SIZE], axis=1)
    marks = jnp.pad(marks.astype(jnp.bfloat16), ((0, 0), (0, HEAD_SIZE - 2)))

    half = HEAD_SIZE // 2
    freq = 10000.0 ** (-(jnp.arange(half, dtype=jnp.float32) * 2.0 / HEAD_SIZE))
    where = (positions[:, None] + step[None, :]).reshape(rows)
    angle = where[:, None].astype(jnp.float32) * freq
    cosine, sine = jnp.cos(angle), jnp.sin(angle)
    cosine = jnp.concatenate([cosine, cosine], axis=1)
    sine = jnp.concatenate([-sine, sine], axis=1)

    key_rows = rotated_prefix_keys[0]
    value_rows = shared_prefix_values[0]
    results, backs, own = [], [], []
    asked_first = far = None
    for i, (first, heads) in enumerate(zip(firsts, chunks, strict=True)):
        if staged:
            products = project(
                index, weights, mine, other, [settle(weights[6:], SETTLE)] if i == 0 and SETTLE else []
            )
            if i + 1 < len(chunks):
                started = first_round(weight_columns(i + 1), owners, weights[3:5])
                weights = second_round(started, owners)
            if i > 0 and TINY1:
                products = [products[0]] + [behind(p, before) for p in products[1:3]] + [products[3]]
            parts = line_sums(products, owners, inner, RS[min(i, 1)])
            if i + 1 < len(chunks):
                parts = after(parts, *weights)
        else:
            piece = qkv_weight[:, first * unit : (first + heads) * unit]
            parts = project_any(tokens, piece, owners, inner)
        if far is not None:
            if FARGATE:
                parts, far = lax.optimization_barrier((parts, far))
            backs.append(exchange(far.reshape(owners, capacity * DECODE_STEPS, -1)))
        packed, query, own_key, own_value = pack(
            parts, cosine, sine, route, marks, heads, int(first == 0)
        )
        own.append(near_part(query, own_key, own_value))
        before = passed_on(packed)
        if staged and PGATE:
            packed, weights = lax.optimization_barrier((packed, weights))
        width = packed.shape[1]
        asked = exchange(packed.reshape(owners, capacity * DECODE_STEPS, width))
        asked = asked.reshape(slots * DECODE_STEPS, width)
        asked_first = asked if first == 0 else asked_first
        far = prefix_part(asked, asked_first, key_rows, value_rows, first, heads)
    backs.append(exchange(far.reshape(owners, capacity * DECODE_STEPS, -1)))
    for back, kept in zip(backs, own, strict=True):
        results.append(join(back.reshape(slots * DECODE_STEPS, -1), route, *kept))
    return jnp.concatenate(results, axis=1).reshape(rows_dev, DECODE_STEPS, -1)


def solution(mesh):
    return jax.shard_map(
        on_device,
        mesh=mesh,
        in_specs=(
            P("wide", None, "narrow"),
            P("wide", "narrow"),
            P("wide", None, "narrow"),
            P("wide", None, "narrow"),
            P("wide", None),
            P("wide"),
        ),
        out_specs=P("wide", None, "narrow"),
        check_vma=False,
    )
```

```python
import functools

import jax
import jax.numpy as jnp
from jax import lax
from jax.experimental import pallas as pl
from jax.experimental.pallas import tpu as pltpu
from jax.sharding import PartitionSpec as P

QUERY_HEADS = 32
KEY_VALUE_HEADS = 8
HEAD_SIZE = 128
DECODE_STEPS = 2
GROUP = QUERY_HEADS // KEY_VALUE_HEADS
SCALE = 1.0 / HEAD_SIZE**0.5
LOG2E = 1.4426950408889634
FLOOR = 512
SETTLE = 20_000_000
CHUNKS = (2, 2)
PIECES = 3
NT = (((1,), (1,)), ((), ()))
NN = (((1,), (0,)), ((), ()))


def dot(left, right, dims=NN):
    return lax.dot_general(left, right, dims, preferred_element_type=jnp.float32)


def whole_specs(count):
    return [pl.BlockSpec(memory_space=pltpu.VMEM)] * count


def prefix_kernel(tile, heads, asked, marks, keys, values, out):
    rows = asked.shape[0]
    length = keys.shape[0]
    head = pl.program_id(0)
    wide = heads * GROUP * HEAD_SIZE
    bound = (marks[:, 0:1].astype(jnp.float32) + marks[:, 1:2].astype(jnp.float32)).astype(jnp.int32)
    lane = lax.broadcasted_iota(jnp.int32, (rows, HEAD_SIZE), 1)

    @pl.when(head == 0)
    def _():
        out[:, wide:] = jnp.zeros((rows, HEAD_SIZE), out.dtype)

    stat = out[:, wide:].astype(jnp.float32)
    ones = jnp.ones((tile, HEAD_SIZE), jnp.bfloat16)
    for member in range(GROUP):
        column = head * GROUP + member
        at = pl.ds(pl.multiple_of(column * HEAD_SIZE, HEAD_SIZE), HEAD_SIZE)
        query = asked[:, at]
        parts = []
        top = None
        for start in range(0, length, tile):
            score = dot(query, keys[start : start + tile, :], NT)
            if start + tile > FLOOR:
                where = start + lax.broadcasted_iota(jnp.int32, score.shape, 1)
                score = jnp.where(where < bound, score, -1e30)
            parts.append(score)
            high = jnp.max(score, axis=1, keepdims=True)
            top = high if top is None else jnp.maximum(top, high)
        total = jnp.zeros((rows, 1), jnp.float32)
        summed = jnp.zeros((rows, HEAD_SIZE), jnp.float32)
        for index, start in enumerate(range(0, length, tile)):
            weight = jnp.exp2((parts[index] - top) * (SCALE * LOG2E)).astype(jnp.bfloat16)
            both = dot(weight, jnp.concatenate([values[start : start + tile, :], ones], axis=1))
            summed = summed + both[:, :HEAD_SIZE]
            total = total + both[:, HEAD_SIZE : HEAD_SIZE + 1]
        out[:, at] = (summed / total).astype(jnp.bfloat16)
        left = top * SCALE + jnp.log(total)
        for piece in range(PIECES):
            part = left.astype(jnp.bfloat16).astype(jnp.float32)
            stat = jnp.where(lane == piece * heads * GROUP + column, part, stat)
            left = left - part
    out[:, wide:] = stat.astype(jnp.bfloat16)


def prefix_part(asked, marks, keys, values, first, heads):
    rows = asked.shape[0]
    length = keys.shape[0]
    wide = heads * GROUP * HEAD_SIZE
    last = marks.shape[1] // HEAD_SIZE - 1
    block = pl.BlockSpec((length, HEAD_SIZE), lambda i: (0, first + i))
    return pl.pallas_call(
        functools.partial(prefix_kernel, min(length, 256), heads),
        grid=(heads,),
        out_shape=jax.ShapeDtypeStruct((rows, wide + HEAD_SIZE), jnp.bfloat16),
        in_specs=[
            pl.BlockSpec((rows, wide), lambda i: (0, 0)),
            pl.BlockSpec((rows, HEAD_SIZE), lambda i: (0, last)),
            block,
            block,
        ],
        out_specs=pl.BlockSpec((rows, wide + HEAD_SIZE), lambda i: (0, 0)),
        compiler_params=pltpu.CompilerParams(vmem_limit_bytes=40 * 2**20),
        cost_estimate=pl.CostEstimate(
            flops=4 * rows * length * wide,
            bytes_accessed=4 * length * heads * HEAD_SIZE,
            transcendentals=rows * length * heads * GROUP,
        ),
        name="prefix_part",
    )(asked, marks, keys, values)


def pack_kernel(count, *refs):
    parts, (cosine, sine, route, marks, asked, query, key, value) = refs[:count], refs[count:]
    heads = key.shape[1] // HEAD_SIZE

    def column(index):
        at = slice(index * HEAD_SIZE, (index + 1) * HEAD_SIZE)
        total = parts[0][:, at].astype(jnp.float32)
        for part in parts[1:]:
            total = total + part[:, at].astype(jnp.float32)
        return total

    def rotated(block):
        turned = pltpu.roll(block, HEAD_SIZE // 2, 1)
        return (block * cosine[...] + turned * sine[...]).astype(jnp.bfloat16)

    for head in range(heads):
        base = head * (GROUP + 2)
        for member in range(GROUP):
            at = head * GROUP + member
            query[:, at * HEAD_SIZE : (at + 1) * HEAD_SIZE] = rotated(column(base + member))
        at = slice(head * HEAD_SIZE, (head + 1) * HEAD_SIZE)
        key[:, at] = rotated(column(base + GROUP))
        value[:, at] = column(base + GROUP + 1).astype(jnp.bfloat16)
    wide = query.shape[1]
    asked[:, :wide] = dot(route[...], query[...]).astype(jnp.bfloat16)
    if asked.shape[1] > wide:
        asked[:, wide:] = dot(route[...], marks[...]).astype(jnp.bfloat16)


def pack(parts, cosine, sine, route, marks, heads, marked):
    rows = cosine.shape[0]
    slots = route.shape[0]
    wide_q, wide_k = heads * GROUP * HEAD_SIZE, heads * HEAD_SIZE
    return pl.pallas_call(
        functools.partial(pack_kernel, len(parts)),
        out_shape=[
            jax.ShapeDtypeStruct((slots, wide_q + marked * HEAD_SIZE), jnp.bfloat16),
            jax.ShapeDtypeStruct((rows, wide_q), jnp.bfloat16),
            jax.ShapeDtypeStruct((rows, wide_k), jnp.bfloat16),
            jax.ShapeDtypeStruct((rows, wide_k), jnp.bfloat16),
        ],
        in_specs=whole_specs(len(parts) + 4),
        out_specs=whole_specs(4),
        compiler_params=pltpu.CompilerParams(vmem_limit_bytes=24 * 2**20),
        cost_estimate=pl.CostEstimate(
            flops=2 * slots * rows * wide_q, bytes_accessed=8 * rows * wide_q, transcendentals=0
        ),
        name="pack",
    )(*parts, cosine, sine, route, marks)


def near_kernel(query, key, value, summed, stat):
    rows = query.shape[0]
    heads = key.shape[1] // HEAD_SIZE
    lane = lax.broadcasted_iota(jnp.int32, (rows, HEAD_SIZE), 1)
    kept = jnp.zeros((rows, HEAD_SIZE), jnp.float32)
    row = lax.broadcasted_iota(jnp.int32, (rows, rows), 0)
    other = lax.broadcasted_iota(jnp.int32, (rows, rows), 1)
    allowed = (row // DECODE_STEPS == other // DECODE_STEPS) & (other <= row)
    for head in range(heads):
        own = slice(head * HEAD_SIZE, (head + 1) * HEAD_SIZE)
        for member in range(GROUP):
            column = head * GROUP + member
            at = slice(column * HEAD_SIZE, (column + 1) * HEAD_SIZE)
            score = jnp.where(allowed, dot(query[:, at], key[:, own], NT) * SCALE, -1e30)
            top = jnp.max(score, axis=1, keepdims=True)
            weight = jnp.exp(score - top)
            total = jnp.sum(weight, axis=1, keepdims=True)
            summed[:, at] = dot(weight.astype(jnp.bfloat16), value[:, own])
            kept = jnp.where(lane == column, top, kept)
            kept = jnp.where(lane == heads * GROUP + column, total, kept)
    stat[...] = kept


def near_part(query, key, value):
    rows, wide = query.shape
    return pl.pallas_call(
        near_kernel,
        out_shape=[
            jax.ShapeDtypeStruct((rows, wide), jnp.float32),
            jax.ShapeDtypeStruct((rows, HEAD_SIZE), jnp.float32),
        ],
        in_specs=whole_specs(3),
        out_specs=whole_specs(2),
        compiler_params=pltpu.CompilerParams(vmem_limit_bytes=24 * 2**20),
        cost_estimate=pl.CostEstimate(
            flops=4 * rows * rows * wide, bytes_accessed=8 * rows * wide, transcendentals=0
        ),
        name="near_part",
    )(query, key, value)


def join_kernel(back, route, summed, stat, out):
    wide = summed.shape[1]
    columns = wide // HEAD_SIZE
    far = dot(route[...], back[...], (((0,), (0,)), ((), ())))
    marks = far[:, wide:]
    for column in range(columns):
        at = slice(column * HEAD_SIZE, (column + 1) * HEAD_SIZE)
        level = marks[:, column : column + 1]
        for piece in range(1, PIECES):
            lane = piece * columns + column
            level = level + marks[:, lane : lane + 1]
        top = stat[:, column : column + 1]
        total = stat[:, columns + column : columns + column + 1]
        both = jnp.maximum(level, top)
        left = jnp.exp(level - both)
        right = jnp.exp(top - both)
        merged = (far[:, at] * left + summed[:, at] * right) / (left + total * right)
        out[:, at] = merged.astype(jnp.bfloat16)


def join(back, route, summed, stat):
    return pl.pallas_call(
        join_kernel,
        out_shape=jax.ShapeDtypeStruct(summed.shape, jnp.bfloat16),
        in_specs=whole_specs(4),
        out_specs=whole_specs(1)[0],
        compiler_params=pltpu.CompilerParams(vmem_limit_bytes=24 * 2**20),
        cost_estimate=pl.CostEstimate(
            flops=2 * route.shape[0] * route.shape[1] * back.shape[1],
            bytes_accessed=8 * summed.shape[0] * summed.shape[1],
            transcendentals=0,
        ),
        name="join",
    )(back, route, summed, stat)


def project_kernel(index, *refs):
    pieces, mine, other, outs, (rows, weight) = (
        refs[:8], refs[8:12], refs[12:16], refs[-6:-2], refs[-2:]
    )
    half, columns = pieces[0].shape
    size = mine[0].shape[0]
    place, end, holder = index[0], index[1], index[2]
    for i, piece in enumerate(pieces):
        start = (place ^ (i // 2)) * (2 * half) + (i % 2) * half
        weight[pl.ds(pl.multiple_of(start, 16), half), :] = piece[...]

    def fill(source):
        rows[:size] = source[0][...]
        rows[3 * size :] = source[2][...]

        @pl.when(end == 1)
        def _():
            rows[size : 2 * size] = source[3][...]
            rows[2 * size : 3 * size] = source[1][...]

        @pl.when(end == 0)
        def _():
            rows[size : 2 * size] = source[1][...]
            rows[2 * size : 3 * size] = source[3][...]

    @pl.when(holder == 1)
    def _():
        fill(mine)

    @pl.when(holder == 0)
    def _():
        fill(other)

    tile = 256
    for start in range(0, columns, tile):
        result = dot(rows[...], weight[:, start : start + tile]).astype(jnp.bfloat16)
        for i, out in enumerate(outs):
            out[:, start : start + tile] = result[i * size : (i + 1) * size]


def settle_kernel(*refs):
    refs[-1][...] = jnp.zeros_like(refs[-1])


def settle(arrived, size):
    return pl.pallas_call(
        settle_kernel,
        out_shape=jax.ShapeDtypeStruct((8, HEAD_SIZE), jnp.float32),
        in_specs=[pl.BlockSpec(memory_space=pl.ANY)] * len(arrived),
        out_specs=pl.BlockSpec(memory_space=pltpu.VMEM),
        cost_estimate=pl.CostEstimate(flops=0, bytes_accessed=size, transcendentals=0),
        name="settle",
    )(*arrived)


def project(index, pieces, mine, other, marks):
    columns = pieces[0].shape[1]
    size, depth = mine[0].shape
    return pl.pallas_call(
        project_kernel,
        out_shape=[jax.ShapeDtypeStruct((size, columns), jnp.bfloat16)] * 4,
        in_specs=[pl.BlockSpec(memory_space=pltpu.SMEM)]
        + whole_specs(16)
        + [pl.BlockSpec(memory_space=pl.ANY)] * len(marks),
        out_specs=whole_specs(4),
        scratch_shapes=[
            pltpu.VMEM((4 * size, depth), jnp.bfloat16),
            pltpu.VMEM((depth, columns), jnp.bfloat16),
        ],
        compiler_params=pltpu.CompilerParams(vmem_limit_bytes=40 * 2**20),
        cost_estimate=pl.CostEstimate(
            flops=8 * size * depth * columns, bytes_accessed=2 * depth * columns, transcendentals=0
        ),
        name="project",
    )(index, *pieces, *mine, *other, *marks)


def after(value, *done):
    return lax.optimization_barrier((value, *done))[0]


def passed_on(source):
    return lax.ppermute(source[:16, :HEAD_SIZE], "narrow", [(0, 1), (1, 0)])[:1, :1]


def behind(value, mark):
    return jnp.where(mark == mark, value, 0).astype(value.dtype)


def inner_size(owners):
    return 4 if owners % 4 == 0 else 1


def across(block, mask, owners):
    return lax.ppermute(block, "wide", [(i, i ^ mask) for i in range(owners)])


def first_round(piece, owners, gate):
    half = piece.shape[0] // 2
    upper, lower = piece[:half], piece[half:]
    if gate is not None:
        upper, lower = after((upper, lower), *gate)
    return [upper, lower, across(upper, 1, owners), across(lower, 2, owners)]


def second_round(blocks, owners):
    upper, lower, upper_1, lower_2 = blocks
    upper_2, lower_1 = across(upper, 2, owners), across(lower, 1, owners)
    upper_3, lower_3 = across(upper_1, 2, owners), across(lower_2, 1, owners)
    return [upper, lower, upper_1, lower_1, upper_2, lower_2, upper_3, lower_3]


def line_groups(owners, inner):
    return [[i * inner + j for i in range(owners // inner)] for j in range(inner)]


def line_tokens(tokens, owners, inner, gate):
    plane = lax.axis_index("wide") // inner
    rows = tokens.shape[0] * tokens.shape[1]
    flat = tokens.reshape(rows, tokens.shape[2])
    if gate is not None:
        flat = behind(flat, gate)
    width = flat.shape[1] // 2
    even = plane % 2 == 0
    same = jnp.where(even, flat[:, :width], flat[:, width:])
    swap = jnp.where(even, flat[:, width:], flat[:, :width])
    blocks = [same]
    for mask, block in ((1, swap), (2, same), (3, swap)):
        pairs = []
        for owner in range(owners):
            there = owner ^ (mask * inner)
            core = there // inner // 2
            pairs.append((owner * 2 + core, there * 2 + core))
        blocks.append(lax.ppermute(block, ("wide", "narrow"), pairs))
    return blocks


def from_other_core(blocks):
    return [lax.ppermute(block, "narrow", [(0, 1), (1, 0)]) for block in blocks]


def line_sums(partial, owners, inner):
    own, first, second, third = partial
    plane = lax.axis_index("wide") // inner
    end = (plane == 0) | (plane == 3)

    def along(block, hops):
        pairs = [(a * inner + j, b * inner + j) for a, b in hops for j in range(inner)]
        return lax.ppermute(block, "wide", pairs)

    near = along(first, [(0, 1), (1, 0), (2, 3), (3, 2)])
    middle = along(second, [(1, 2), (2, 1)])
    near, middle, second = lax.optimization_barrier((near, middle, second))
    outer = along(second, [(0, 1), (3, 2)])
    passed = jnp.where(end, 0, near.astype(jnp.float32))
    third = (third.astype(jnp.float32) + passed).astype(jnp.bfloat16)
    far = along(third, [(0, 2), (2, 0), (1, 3), (3, 1)])
    near = jnp.where(end, near, 0)
    return [own, near, outer, middle, far]


def project_any(tokens, qkv_weight, owners, inner):
    planes = owners // inner
    rows = tokens.shape[0] * tokens.shape[1]
    flat = lax.all_gather(tokens.reshape(rows, -1), "narrow", axis=1, tiled=True)
    weight = qkv_weight
    if inner > 1:
        groups = [[i * inner + j for j in range(inner)] for i in range(planes)]
        weight = lax.all_gather(weight, "wide", axis=0, tiled=True, axis_index_groups=groups)
    if planes == 1:
        return [dot(flat, weight)]
    lines = line_groups(owners, inner)
    parts = flat.reshape(rows, planes, -1).transpose(1, 0, 2)
    parts = lax.all_to_all(
        parts, "wide", split_axis=0, concat_axis=0, tiled=True, axis_index_groups=lines
    )
    partial = dot(parts.reshape(planes * rows, -1), weight).astype(jnp.bfloat16)
    parts = lax.all_to_all(
        partial.reshape(planes, rows, -1), "wide", split_axis=0, concat_axis=0, tiled=True,
        axis_index_groups=lines,
    )
    return [parts[i] for i in range(planes)]


def exchange(block):
    return lax.all_to_all(block, "wide", split_axis=0, concat_axis=0, tiled=True)


def on_device(tokens, qkv_weight, rotated_prefix_keys, shared_prefix_values, prefix_of, positions):
    rows_dev = tokens.shape[0]
    owners = lax.axis_size("wide")
    halves = lax.axis_size("narrow")
    inner = inner_size(owners)
    rows = rows_dev * DECODE_STEPS
    capacity = max(2, (2 * rows_dev + owners - 1) // owners)
    slots = owners * capacity
    kv_local = rotated_prefix_keys.shape[2] // HEAD_SIZE
    chunks = CHUNKS if sum(CHUNKS) == kv_local else (kv_local,)
    firsts = [sum(chunks[:i]) for i in range(len(chunks))]
    unit = (GROUP + 2) * HEAD_SIZE
    here = lax.axis_index("wide")
    plane = here // inner
    staged = owners == 4 * inner and inner == 4 and halves == 2

    if staged:
        def weight_columns(i):
            return qkv_weight[:, firsts[i] * unit : (firsts[i] + chunks[i]) * unit]

        started = first_round(weight_columns(0), owners, None)
        mine = line_tokens(tokens, owners, inner, passed_on(started[0]))
        weights, other = second_round(started, owners), from_other_core(mine)
        index = jnp.stack(
            [
                here % inner,
                ((plane == 0) | (plane == 3)).astype(jnp.int32),
                (lax.axis_index("narrow") == plane // 2).astype(jnp.int32),
            ]
        ).astype(jnp.int32)

    chosen = prefix_of[:, 0]
    hits = (chosen[:, None] == jnp.arange(owners, dtype=jnp.int32)[None, :]).astype(jnp.int32)
    rank = jnp.sum((jnp.cumsum(hits, axis=0) - hits) * hits, axis=1)
    target = chosen * capacity + rank
    step = jnp.arange(DECODE_STEPS, dtype=jnp.int32)
    line = (target[:, None] * DECODE_STEPS + step[None, :]).reshape(rows)
    route = (
        line[None, :] == jnp.arange(slots * DECODE_STEPS, dtype=jnp.int32)[:, None]
    ).astype(jnp.bfloat16)

    count = jnp.repeat(positions, DECODE_STEPS)
    marks = jnp.stack([count - count % HEAD_SIZE, count % HEAD_SIZE], axis=1)
    marks = jnp.pad(marks.astype(jnp.bfloat16), ((0, 0), (0, HEAD_SIZE - 2)))

    half = HEAD_SIZE // 2
    freq = 10000.0 ** (-(jnp.arange(half, dtype=jnp.float32) * 2.0 / HEAD_SIZE))
    where = (positions[:, None] + step[None, :]).reshape(rows)
    angle = where[:, None].astype(jnp.float32) * freq
    cosine, sine = jnp.cos(angle), jnp.sin(angle)
    cosine = jnp.concatenate([cosine, cosine], axis=1)
    sine = jnp.concatenate([-sine, sine], axis=1)

    key_rows = rotated_prefix_keys[0]
    value_rows = shared_prefix_values[0]
    results, backs, own = [], [], []
    asked_first = far = None
    for i, (first, heads) in enumerate(zip(firsts, chunks, strict=True)):
        if staged:
            products = project(
                index, weights, mine, other, [settle(weights[6:], SETTLE)] if i == 0 else []
            )
            if i + 1 < len(chunks):
                started = first_round(weight_columns(i + 1), owners, weights[3:5])
                weights = second_round(started, owners)
            parts = line_sums(products, owners, inner)
            if i + 1 < len(chunks):
                parts = after(parts, *weights)
        else:
            piece = qkv_weight[:, first * unit : (first + heads) * unit]
            parts = project_any(tokens, piece, owners, inner)
        if far is not None:
            parts, far = lax.optimization_barrier((parts, far))
            backs.append(exchange(far.reshape(owners, capacity * DECODE_STEPS, -1)))
        packed, query, own_key, own_value = pack(
            parts, cosine, sine, route, marks, heads, int(first == 0)
        )
        own.append(near_part(query, own_key, own_value))
        width = packed.shape[1]
        asked = exchange(packed.reshape(owners, capacity * DECODE_STEPS, width))
        asked = asked.reshape(slots * DECODE_STEPS, width)
        asked_first = asked if first == 0 else asked_first
        far = prefix_part(asked, asked_first, key_rows, value_rows, first, heads)
    backs.append(exchange(far.reshape(owners, capacity * DECODE_STEPS, -1)))
    for back, kept in zip(backs, own, strict=True):
        results.append(join(back.reshape(slots * DECODE_STEPS, -1), route, *kept))
    return jnp.concatenate(results, axis=1).reshape(rows_dev, DECODE_STEPS, -1)


def solution(mesh):
    return jax.shard_map(
        on_device,
        mesh=mesh,
        in_specs=(
            P("wide", None, "narrow"),
            P("wide", "narrow"),
            P("wide", None, "narrow"),
            P("wide", None, "narrow"),
            P("wide", None),
            P("wide"),
        ),
        out_specs=P("wide", None, "narrow"),
        check_vma=False,
    )
```
